512 devices in a mesh: cuts: 16 (over y, core), tile: 32 (over z, x).
Axes of the slice: x: 4, y: 8, z: 8, core: 2. Of those that a mesh axis runs over, the one named last changes fastest.
Arguments:
- obj_real: float32 [16, 4096, 256], P('cuts', 'tile'), may hold values from 0.9 to 1.1
- obj_imag: float32 [16, 4096, 256], P('cuts', 'tile'), may hold values from -0.4 to 0.4
- probe_real: float32 [128, 128], replicated, may hold values from -3.5 to 3.5
- probe_imag: float32 [128, 128], replicated, may hold values from -3.5 to 3.5
- prop_phase: float32 [128], replicated, may hold values from -3.140625 to 3.140625
- intensity: float32 [512, 128, 128], P('tile'), may hold values from 0 to 2
- offsets: int32 [512, 2], P('tile'), may hold values from 0 to 128, as said below
- counts: int32 [32], P('tile'), may hold values from 1 to 16, as said below
Outputs:
- object_grad: float32 [2, 16, 4096, 256], P(None, 'cuts', 'tile')
- probe_grad: float32 [2, 128, 128], P(None, 'cuts')
The draws below stay inside these ranges and needn't reach their ends.
Inputs may be any that keep to these rules, and one draw needn't show every extreme that they name: `offsets`: column 0 lies in 0 to 127 and column 1 in 0 to 128; the upper ends are reached in every draw. `counts`: every tile has at least one live slot and some tile has all 16 slots live.
All inputs are finite; a program needn't handle non-finite values.
Results may differ from the reference program's by a relative error of at most 0.0003.
Values sent between devices are 32-bit elements; how exact they have to be, the bound alone decides.
No kernel may reach another device: no remote copies, remote signals or barrier semaphores. Data moves between devices by JAX's collectives and lax.ppermute only.
A program may use at most 64 MiB of HBM per device.

```python
import jax
import jax.numpy as jnp
from jax import lax

PW = 128
TH = 128
W = 256
CAP = 16
TILES = 32
SLICES = 16
ROWS = 4096
POSITIONS = 512


def draw_offsets(key, part):
    key = jax.random.fold_in(key, 23)
    key_rows, key_cols, key_pick = jax.random.split(key, 3)
    total_slots = CAP * TILES
    row_part = jax.random.randint(key_rows, (total_slots,), 0, TH)
    col_part = jax.random.randint(key_cols, (total_slots,), 0, W - PW + 1)
    picks = jax.random.randint(key_pick, (2,), 0, total_slots)
    slot_ids = jnp.arange(total_slots)
    row_part = jnp.where(slot_ids == picks[0], TH - 1, row_part)
    col_part = jnp.where(slot_ids == picks[1], W - PW, col_part)
    return jnp.stack([row_part, col_part], axis=1).astype(jnp.int32)


def draw_counts(key, part):
    key = jax.random.fold_in(key, 11)
    key_base, key_full = jax.random.split(key)
    base_counts = jax.random.randint(key_base, (TILES,), 1, CAP // 2 + 1)
    full_tile = jax.random.randint(key_full, (), 0, TILES)
    return jnp.where(jnp.arange(TILES) == full_tile, CAP, base_counts).astype(jnp.int32)


def levels(rng, extent, shards, low, top_value):
    def one(axis_at, blocks):
        steps = jax.random.uniform(jax.random.fold_in(jax.random.fold_in(rng, 6), axis_at), (blocks,), jnp.float32, low / len(shards), top_value / len(shards))
        return jnp.repeat(jnp.exp(steps), extent[axis_at] // blocks).reshape((-1,) + (1,) * (len(extent) - axis_at - 1))

    loudness = one(*shards[0])
    for cut in shards[1:]:
        loudness = loudness * one(*cut)
    return loudness


def noise(key, extent, spread, reach, cuts=(), kind=jnp.bfloat16):
    factor_of = levels(key, extent, cuts, -0.22, 0.18) if cuts else 1.0
    array = jax.random.normal(key, extent, jnp.float32) * spread * factor_of
    return jnp.minimum(jnp.maximum(array, -reach), reach).astype(kind)


def setup_inputs(seed: int = 0) -> dict:
    streams_of = jax.random.split(jax.random.key(seed), 9)
    return {
        "obj_real": jnp.clip(1.0 + 0.02 * jax.random.normal(streams_of[0], (SLICES, ROWS, W), jnp.float32), 0.9, 1.1),
        "obj_imag": noise(streams_of[1], (SLICES, ROWS, W), 0.1, 0.4, ((0, 16), (1, 32)), jnp.float32),
        "probe_real": noise(streams_of[2], (PW, PW), 0.7, 3.5, (), jnp.float32),
        "probe_imag": noise(streams_of[3], (PW, PW), 0.7, 3.5, (), jnp.float32),
        "prop_phase": jnp.clip(jax.random.uniform(streams_of[4], (PW,), jnp.float32, -3.140625, 3.140625), -3.140625, 3.140625),
        "intensity": jnp.clip(2.0 * jax.random.uniform(streams_of[5], (POSITIONS, PW, PW), jnp.float32) ** levels(streams_of[5], (POSITIONS, PW, PW), ((0, 32),), -0.2, 0.2), 0.0, 2.0),
        "offsets": draw_offsets(jax.random.fold_in(streams_of[8], 71), 0),
        "counts": draw_counts(jax.random.fold_in(streams_of[8], 71), 0),
    }


def reference(obj_real, obj_imag, probe_real, probe_imag, prop_phase, intensity, offsets, counts):
    slice_count = obj_real.shape[0]
    total_rows = obj_real.shape[1]
    patch_width = probe_real.shape[0]
    obj_full = lax.complex(obj_real, obj_imag)
    obj_wrap = jnp.concatenate([obj_full, obj_full[:, :patch_width]], axis=1)
    probe = lax.complex(probe_real, probe_imag)
    kernel = lax.complex(jnp.cos(prop_phase), jnp.sin(prop_phase))
    transfer = kernel[:, None] * kernel[None, :]
    zero_index = jnp.zeros((), jnp.int32)

    def propagate(current):
        return jnp.fft.ifft2(jnp.fft.fft2(current) * transfer)

    def back_propagate(current):
        return jnp.fft.ifft2(jnp.fft.fft2(current) * jnp.conj(transfer))

    def one_position(loop_state, position):
        gradients, probe_sum = loop_state
        tile_index = position // CAP
        live_weight = (position % CAP < counts[tile_index]).astype(obj_real.dtype)
        row_start = (tile_index * TH + offsets[position, 0]).astype(jnp.int32)
        col_start = offsets[position, 1].astype(jnp.int32)
        patches = lax.dynamic_slice(obj_wrap, (zero_index, row_start, col_start), (slice_count, patch_width, patch_width))
        wave_list = []
        current = probe
        for slice_index in range(slice_count):
            wave_list.append(current)
            current = propagate(current * patches[slice_index])
        far_field = jnp.fft.fft2(current, norm="ortho")
        excess = 2.0 * (jnp.real(far_field) * jnp.real(far_field) + jnp.imag(far_field) * jnp.imag(far_field) - intensity[position])
        adjoint = jnp.fft.ifft2(excess * far_field, norm="ortho")
        grad_list = [None] * slice_count
        for slice_index in reversed(range(slice_count)):
            inner_grad = back_propagate(adjoint)
            grad_list[slice_index] = jnp.conj(wave_list[slice_index]) * inner_grad
            adjoint = jnp.conj(patches[slice_index]) * inner_grad
        patch_grads = jnp.stack(grad_list) * live_weight
        region = lax.dynamic_slice(gradients, (zero_index, row_start, col_start), (slice_count, patch_width, patch_width))
        gradients = lax.dynamic_update_slice(gradients, region + patch_grads, (zero_index, row_start, col_start))
        return (gradients, probe_sum + adjoint * live_weight), None

    initial_state = (jnp.zeros(obj_wrap.shape, obj_wrap.dtype), jnp.zeros(probe.shape, probe.dtype))
    final_state = lax.scan(one_position, initial_state, jnp.arange(CAP * TILES, dtype=jnp.int32))[0]
    gradients, probe_sum = final_state
    folded = gradients[:, :total_rows].at[:, :patch_width].add(gradients[:, total_rows:])
    object_grad = jnp.stack([jnp.real(folded), jnp.imag(folded)])
    probe_grad = jnp.stack([jnp.real(probe_sum), jnp.imag(probe_sum)])
    return object_grad, probe_grad
```

```python
import functools
import math

import jax
import jax.numpy as jnp
import numpy as np
from jax import lax
from jax.experimental import pallas as pl
from jax.experimental.pallas import tpu as pltpu
from jax.sharding import PartitionSpec as P

VMEM = pltpu.VMEM
SMEM = pltpu.SMEM


def split_bf16(value):
    high = value.astype(jnp.bfloat16)
    low = (value - high.astype(jnp.float32)).astype(jnp.bfloat16)
    return high, low


def exact_dot(left, right):
    return jnp.dot(left, right, precision=lax.Precision.HIGHEST, preferred_element_type=jnp.float32)


def fourier_pair(size):
    places = np.arange(size)
    angle = (places[:, None] * places[None, :] % size) * (2.0 * math.pi / size)
    scale = 1.0 / math.sqrt(size)
    return (np.cos(angle) * scale).astype(np.float32), (-np.sin(angle) * scale).astype(np.float32)


def right_operator(real, imag):
    return jnp.concatenate(
        [jnp.concatenate([real, imag], axis=1), jnp.concatenate([-imag, real], axis=1)], axis=0
    )


def left_operator(real, imag):
    return jnp.concatenate(
        [jnp.concatenate([real, -imag], axis=1), jnp.concatenate([imag, real], axis=1)], axis=0
    )


def rounded_split(matrix):
    high = lax.reduce_precision(matrix, 8, 7)
    return high.astype(jnp.bfloat16), (matrix - high).astype(jnp.bfloat16)


def stacked_right(matrix):
    high, low = rounded_split(matrix)
    return jnp.concatenate([high, high, low], axis=0)


def stacked_left(matrix):
    high, low = rounded_split(matrix)
    return jnp.concatenate([high, high, low], axis=1)


def build_operators(prop_phase):
    size = prop_phase.shape[0]
    f_real, f_imag = fourier_pair(size)
    k_real = jnp.cos(prop_phase)[None, :]
    k_imag = jnp.sin(prop_phase)[None, :]
    l_real = f_real * k_real + f_imag * k_imag
    l_imag = f_real * k_imag - f_imag * k_real
    s_real = exact_dot(l_real, f_real) - exact_dot(l_imag, f_imag)
    s_imag = exact_dot(l_real, f_imag) + exact_dot(l_imag, f_real)
    rights = jnp.stack(
        [
            stacked_right(right_operator(s_real.T, s_imag.T)),
            stacked_right(right_operator(f_real, f_imag)),
            stacked_right(right_operator(f_real, -f_imag)),
            stacked_right(right_operator(s_real, -s_imag)),
        ]
    )
    lefts = jnp.stack(
        [
            stacked_left(left_operator(s_real, s_imag)),
            stacked_left(left_operator(f_real, f_imag)),
            stacked_left(left_operator(f_real, -f_imag)),
            stacked_left(left_operator(s_real.T, -s_imag.T)),
        ]
    )
    return rights, lefts


def sandwich(wide, right, left, size):
    high, low = split_bf16(wide)
    middle = jnp.dot(
        jnp.concatenate([high, low, high], axis=1), right, preferred_element_type=jnp.float32
    )
    tall = jnp.concatenate([middle[:, :size], middle[:, size:]], axis=0)
    high, low = split_bf16(tall)
    out = jnp.dot(
        left, jnp.concatenate([high, low, high], axis=0), preferred_element_type=jnp.float32
    )
    return out[:size], out[size:]


def chain_kernel(live_ref, probe_ref, right_ref, left_ref, window_ref, measured_ref, out_ref, waves):
    slices = window_ref.shape[0]
    size = probe_ref.shape[1]
    extra = size // slices
    live = live_ref[0] > 0

    @pl.when(jnp.logical_not(live))
    def _():
        out_ref[...] = jnp.zeros_like(out_ref)

    @pl.when(live)
    def _():
        def modulated(s, real, imag):
            waves[s, :size, :] = real
            waves[s, size:, :] = imag
            p_real = window_ref[s, :size, :]
            p_imag = window_ref[s, size:, :]
            return jnp.concatenate(
                [real * p_real - imag * p_imag, real * p_imag + imag * p_real], axis=1
            )

        def forward(s, state):
            return sandwich(modulated(s, *state), right_ref[0], left_ref[0], size)

        state = lax.fori_loop(0, slices - 1, forward, (probe_ref[0], probe_ref[1]))
        wide = modulated(slices - 1, *state)
        far_r, far_i = sandwich(wide, right_ref[1], left_ref[1], size)
        excess = 2.0 * (far_r * far_r + far_i * far_i - measured_ref[0])
        wide = jnp.concatenate([excess * far_r, excess * far_i], axis=1)
        inner = sandwich(wide, right_ref[2], left_ref[2], size)

        def deposit(s, h_r, h_i):
            w_r = waves[s, :size, :]
            w_i = waves[s, size:, :]
            p_real = window_ref[s, :size, :]
            p_imag = window_ref[s, size:, :]
            out_ref[s, :size, :] = w_r * h_r + w_i * h_i
            out_ref[s, size : 2 * size, :] = w_r * h_i - w_i * h_r
            return p_real * h_r + p_imag * h_i, p_real * h_i - p_imag * h_r

        def backward(k, state):
            g_r, g_i = deposit(slices - 1 - k, *state)
            return sandwich(
                jnp.concatenate([g_r, g_i], axis=1), right_ref[3], left_ref[3], size
            )

        inner = lax.fori_loop(0, slices - 1, backward, inner)
        g_r, g_i = deposit(0, *inner)
        for s in range(slices):
            out_ref[s, 2 * size : 2 * size + extra, :] = g_r[s * extra : (s + 1) * extra]
            out_ref[s, 2 * size + extra :, :] = g_i[s * extra : (s + 1) * extra]


def run_chain(live, probe, rights, lefts, windows, measured):
    slices, _, size = windows.shape
    rows = 2 * size + 2 * (size // slices)
    vmem = pl.BlockSpec(memory_space=VMEM)
    return pl.pallas_call(
        chain_kernel,
        out_shape=jax.ShapeDtypeStruct((slices, rows, size), jnp.float32),
        in_specs=[pl.BlockSpec(memory_space=SMEM)] + [vmem] * 5,
        out_specs=vmem,
        scratch_shapes=[VMEM((slices, 2 * size, size), jnp.float32)],
        compiler_params=pltpu.CompilerParams(vmem_limit_bytes=40 * 2**20),
        name="chain",
    )(live, probe, rights, lefts, windows, measured)


def cut_kernel(offset_ref, real_ref, imag_ref, below_ref, out_ref, region):
    slots = out_ref.shape[0]
    size = out_ref.shape[2]
    rows = real_ref.shape[1]
    for half in range(2):
        cols = pl.ds(half * size, size)
        region[0, half, :rows, :] = real_ref[0, :, cols]
        region[1, half, :rows, :] = imag_ref[0, :, cols]
        region[0, half, rows:, :] = below_ref[0, :, cols]
        region[1, half, rows:, :] = below_ref[1, :, cols]
    lane = lax.broadcasted_iota(jnp.int32, (size, size), 1)

    def one_slot(n, carry):
        row = offset_ref[n, 0]
        col = offset_ref[n, 1]
        shift = lax.rem(size - col + size, size)
        from_first = lane < size - col
        for part in range(2):
            first = pltpu.roll(region[part, 0, pl.ds(row, size), :], shift, 1)
            second = pltpu.roll(region[part, 1, pl.ds(row, size), :], shift, 1)
            out_ref[n, part * size : (part + 1) * size, :] = jnp.where(from_first, first, second)
        return carry

    lax.fori_loop(0, slots, one_slot, 0)


def cut_windows(offsets, obj_real, obj_imag, below, size):
    slots = offsets.shape[0]
    rows, width = obj_real.shape[1:]
    vmem = pl.BlockSpec(memory_space=VMEM)
    return pl.pallas_call(
        cut_kernel,
        out_shape=jax.ShapeDtypeStruct((slots, 2 * size, size), jnp.float32),
        in_specs=[pl.BlockSpec(memory_space=SMEM)] + [vmem] * 3,
        out_specs=vmem,
        scratch_shapes=[VMEM((2, 2, rows + size, size), jnp.float32)],
        compiler_params=pltpu.CompilerParams(vmem_limit_bytes=24 * 2**20),
        name="cut",
    )(offsets, obj_real, obj_imag, below)


def gather_kernel(offset_ref, terms_ref, own_ref, band_ref, probe_ref, region):
    slots, tall, size = terms_ref.shape
    rows = own_ref.shape[1]
    extra = (tall - 2 * size) // 2
    region[...] = jnp.zeros_like(region)
    lane = lax.broadcasted_iota(jnp.int32, (size, size), 1)

    def one_slot(n, total):
        here = pl.ds(offset_ref[n, 0], size)
        col = offset_ref[n, 1]
        in_first = lane >= col
        for part in range(2):
            term = terms_ref[n, part * size : (part + 1) * size, :]
            turned = pltpu.roll(term, lax.rem(col, size), 1)
            region[part, 0, here, :] = region[part, 0, here, :] + jnp.where(in_first, turned, 0.0)
            region[part, 1, here, :] = region[part, 1, here, :] + jnp.where(in_first, 0.0, turned)
        return total + terms_ref[n, 2 * size :, :]

    total = lax.fori_loop(0, slots, one_slot, jnp.zeros((2 * extra, size), jnp.float32))
    for half in range(2):
        cols = pl.ds(half * size, size)
        own_ref[:, :, cols] = region[:, half, :rows, :]
        band_ref[:, :, cols] = region[:, half, rows:, :]
    probe_ref[...] = total


def add_windows(offsets, terms, rows, width):
    slots, tall, size = terms.shape
    vmem = pl.BlockSpec(memory_space=VMEM)
    return pl.pallas_call(
        gather_kernel,
        out_shape=[
            jax.ShapeDtypeStruct((2, rows, width), jnp.float32),
            jax.ShapeDtypeStruct((2, size, width), jnp.float32),
            jax.ShapeDtypeStruct((tall - 2 * size, size), jnp.float32),
        ],
        in_specs=[pl.BlockSpec(memory_space=SMEM), vmem],
        out_specs=[vmem] * 3,
        scratch_shapes=[VMEM((2, 2, rows + size, size), jnp.float32)],
        compiler_params=pltpu.CompilerParams(vmem_limit_bytes=24 * 2**20),
        name="gather",
    )(offsets, terms)


def passed_along(block, axis, distance):
    count = lax.axis_size(axis)
    return lax.ppermute(block, axis, [((i - distance) % count, i) for i in range(count)])


def per_device(obj_real, obj_imag, probe_real, probe_imag, prop_phase, intensity, offsets, counts):
    size = probe_real.shape[0]
    rows, width = obj_real.shape[1:]
    slot = lax.axis_index("cuts")
    below = passed_along(jnp.concatenate([obj_real, obj_imag]), "tile", -1)
    rights, lefts = build_operators(prop_phase)
    probe = jnp.stack([probe_real, probe_imag])
    measured = lax.dynamic_slice_in_dim(intensity, slot, 1, 0)
    live = (slot < counts).astype(jnp.int32)
    windows = cut_windows(offsets, obj_real, obj_imag, below, size)
    windows = lax.all_to_all(windows, "cuts", 0, 0, tiled=True)
    terms = run_chain(live, probe, rights, lefts, windows, measured)
    terms = lax.all_to_all(terms, "cuts", 0, 0, tiled=True)
    own, band, probe_part = add_windows(offsets, terms, rows, width)
    band = passed_along(band, "tile", 1)
    tiles = lax.axis_size("tile")
    spread = jnp.broadcast_to(probe_part[None], (tiles,) + probe_part.shape)
    probe_parts = lax.all_to_all(spread, "tile", 0, 0, tiled=True)
    probe_grad = jnp.sum(probe_parts, axis=0).reshape(2, -1, size)
    object_grad = (own + band)[:, None]
    return object_grad, probe_grad


def solution(mesh):
    in_specs = (
        P("cuts", "tile", None),
        P("cuts", "tile", None),
        P(),
        P(),
        P(),
        P("tile", None, None),
        P("tile", None),
        P("tile"),
    )
    out_specs = (P(None, "cuts", "tile", None), P(None, "cuts", None))
    return jax.shard_map(
        per_device, mesh=mesh, in_specs=in_specs, out_specs=out_specs, check_vma=False
    )
```

```python
import functools
import math

import jax
import jax.numpy as jnp
import numpy as np
from jax import lax
from jax.experimental import pallas as pl
from jax.experimental.pallas import tpu as pltpu
from jax.sharding import PartitionSpec as P

VMEM = pltpu.VMEM
SMEM = pltpu.SMEM


def split_bf16(value):
    high = value.astype(jnp.bfloat16)
    low = (value - high.astype(jnp.float32)).astype(jnp.bfloat16)
    return high, low


def exact_dot(left, right):
    return jnp.dot(left, right, precision=lax.Precision.HIGHEST, preferred_element_type=jnp.float32)


def fourier_pair(size):
    places = np.arange(size)
    angle = (places[:, None] * places[None, :] % size) * (2.0 * math.pi / size)
    scale = 1.0 / math.sqrt(size)
    return (np.cos(angle) * scale).astype(np.float32), (-np.sin(angle) * scale).astype(np.float32)


def rounded_split(matrix, seed):
    high = lax.reduce_precision(matrix, 8, 7)
    dither = np.random.default_rng(seed).uniform(-1.0, 1.0, matrix.shape) * 0.003
    low = (matrix - high) * (1.0 + dither).astype(np.float32)
    return high.astype(jnp.bfloat16), low.astype(jnp.bfloat16)


def build_matrices(prop_phase):
    size = prop_phase.shape[0]
    f_real, f_imag = fourier_pair(size)
    k_real = jnp.cos(prop_phase)[None, :]
    k_imag = jnp.sin(prop_phase)[None, :]
    l_real = f_real * k_real + f_imag * k_imag
    l_imag = f_real * k_imag - f_imag * k_real
    s_real = exact_dot(l_real, f_real) - exact_dot(l_imag, f_imag)
    s_imag = exact_dot(l_real, f_imag) + exact_dot(l_imag, f_real)
    return rounded_split(jnp.stack([s_real, s_imag, s_real.T, s_imag.T, f_real, f_imag]), 1)


def assemble(matrix_ref, right_ref, left_ref):
    size = matrix_ref.shape[1]
    uses = ((0, 2, 1.0), (4, 4, 1.0), (4, 4, -1.0), (2, 0, -1.0))
    for which, (left, right, sign) in enumerate(uses):
        real, imag = matrix_ref[right], matrix_ref[right + 1] * sign
        right_ref[which, :size, :size] = real
        right_ref[which, :size, size:] = imag
        right_ref[which, size:, :size] = -imag
        right_ref[which, size:, size:] = real
        left_ref[which, :, :size] = matrix_ref[left]
        left_ref[which, :, size:] = matrix_ref[left + 1] * sign


def sandwich(wide, operators, which):
    dot = functools.partial(jnp.dot, preferred_element_type=jnp.float32)
    right_high, right_low, left_high, left_low = (ref[which] for ref in operators)
    size = wide.shape[0]
    high, low = split_bf16(wide)
    middle = dot(high, right_high) + dot(low, right_high) + dot(high, right_low)
    swapped = jnp.concatenate([-middle[:, size:], middle[:, :size]], axis=1)
    high, low = split_bf16(jnp.concatenate([middle, swapped], axis=0))
    out = dot(left_high, high) + dot(left_low, high) + dot(left_high, low)
    return out[:, :size], out[:, size:]


def chain_kernel(live_ref, probe_ref, *refs):
    high_ref, low_ref, measured_ref, window_ref, out_ref, waves, *operators = refs
    slices = window_ref.shape[0]
    size = probe_ref.shape[1]
    extra = size // slices
    live = live_ref[0] > 0

    @pl.when(jnp.logical_not(live))
    def _():
        out_ref[...] = jnp.zeros_like(out_ref)

    @pl.when(live)
    def _():
        assemble(high_ref, operators[0], operators[2])
        assemble(low_ref, operators[1], operators[3])

        def modulated(s, real, imag):
            waves[s, :size, :] = real
            waves[s, size:, :] = imag
            p_real = window_ref[s, :size, :]
            p_imag = window_ref[s, size:, :]
            return jnp.concatenate(
                [real * p_real - imag * p_imag, real * p_imag + imag * p_real], axis=1
            )

        state = (probe_ref[0], probe_ref[1])
        for s in range(slices - 1):
            state = sandwich(modulated(s, *state), operators, 0)
        wide = modulated(slices - 1, *state)
        far_r, far_i = sandwich(wide, operators, 1)
        excess = 2.0 * (far_r * far_r + far_i * far_i - measured_ref[0])
        wide = jnp.concatenate([excess * far_r, excess * far_i], axis=1)
        h_r, h_i = sandwich(wide, operators, 2)
        for s in reversed(range(slices)):
            w_r = waves[s, :size, :]
            w_i = waves[s, size:, :]
            p_real = window_ref[s, :size, :]
            p_imag = window_ref[s, size:, :]
            out_ref[s, :size, :] = w_r * h_r + w_i * h_i
            out_ref[s, size : 2 * size, :] = w_r * h_i - w_i * h_r
            g_r = p_real * h_r + p_imag * h_i
            g_i = p_real * h_i - p_imag * h_r
            if s > 0:
                wide = jnp.concatenate([g_r, g_i], axis=1)
                h_r, h_i = sandwich(wide, operators, 3)
        for s in range(slices):
            out_ref[s, 2 * size : 2 * size + extra, :] = g_r[s * extra : (s + 1) * extra]
            out_ref[s, 2 * size + extra :, :] = g_i[s * extra : (s + 1) * extra]


def run_chain(live, probe, matrices, windows, measured):
    slices, _, size = windows.shape
    rows = 2 * size + 2 * (size // slices)
    vmem = pl.BlockSpec(memory_space=VMEM)
    return pl.pallas_call(
        chain_kernel,
        out_shape=jax.ShapeDtypeStruct((slices, rows, size), jnp.float32),
        in_specs=[pl.BlockSpec(memory_space=SMEM)] + [vmem] * 5,
        out_specs=vmem,
        scratch_shapes=[
            VMEM((slices, 2 * size, size), jnp.float32),
            VMEM((4, 2 * size, 2 * size), jnp.bfloat16),
            VMEM((4, 2 * size, 2 * size), jnp.bfloat16),
            VMEM((4, size, 2 * size), jnp.bfloat16),
            VMEM((4, size, 2 * size), jnp.bfloat16),
        ],
        compiler_params=pltpu.CompilerParams(vmem_limit_bytes=16 * 2**20),
        name="chain",
    )(live, probe, *matrices, measured, windows)


def cut_kernel(
    offset_ref, real_hbm, imag_hbm, real_below, imag_below, out_hbm, region, out_ref, sems, out_sems
):
    slots, _, size = out_ref.shape
    rows = real_hbm.shape[1]
    parts = ((0, 0, real_hbm), (1, 0, imag_hbm), (0, rows, real_below), (1, rows, imag_below))
    arrivals = []
    for part, first, source in parts:
        for half in range(2):
            arrivals.append(
                pltpu.make_async_copy(
                    source.at[0, :, pl.ds(half * size, size)],
                    region.at[part, half, pl.ds(first, rows)],
                    sems.at[len(arrivals)],
                )
            )
    for arrival in arrivals:
        arrival.start()
    for arrival in arrivals:
        arrival.wait()
    lane = lax.broadcasted_iota(jnp.int32, (size, size), 1)

    def one_slot(n, carry):
        here = pl.ds(offset_ref[n, 0], size)
        col = offset_ref[n, 1]
        shift = lax.rem(size - col + size, size)
        in_first = lane >= col
        for part in range(2):
            mixed = jnp.where(in_first, region[part, 0, here, :], region[part, 1, here, :])
            out_ref[n, part * size : (part + 1) * size, :] = pltpu.roll(mixed, shift, 1)
        pltpu.make_async_copy(out_ref.at[n], out_hbm.at[n], out_sems.at[n]).start()
        return carry

    lax.fori_loop(0, slots, one_slot, 0, unroll=2)
    for n in range(slots):
        pltpu.make_async_copy(out_ref.at[n], out_hbm.at[n], out_sems.at[n]).wait()


def cut_windows(offsets, obj_real, obj_imag, below_real, below_imag, size):
    slots = offsets.shape[0]
    _, rows, width = obj_real.shape
    return pl.pallas_call(
        cut_kernel,
        out_shape=jax.ShapeDtypeStruct((slots, 2 * size, size), jnp.float32),
        in_specs=[pl.BlockSpec(memory_space=SMEM)] + [pl.BlockSpec(memory_space=pl.ANY)] * 4,
        out_specs=pl.BlockSpec(memory_space=pl.ANY),
        scratch_shapes=[
            VMEM((2, 2, 2 * rows, size), jnp.float32),
            VMEM((slots, 2 * size, size), jnp.float32),
            pltpu.SemaphoreType.DMA((8,)),
            pltpu.SemaphoreType.DMA((slots,)),
        ],
        compiler_params=pltpu.CompilerParams(vmem_limit_bytes=60 * 2**20),
        name="cut",
    )(offsets, obj_real, obj_imag, below_real, below_imag)


def gather_kernel(offset_ref, terms_ref, own_ref, band_ref, region):
    slots, _, size = terms_ref.shape
    rows = own_ref.shape[1]
    region[...] = jnp.zeros_like(region)
    lane = lax.broadcasted_iota(jnp.int32, (size, size), 1)

    def one_slot(n, carry):
        here = pl.ds(offset_ref[n, 0], size)
        col = offset_ref[n, 1]
        in_first = lane >= col
        for part in range(2):
            term = terms_ref[n, part * size : (part + 1) * size, :]
            turned = pltpu.roll(term, lax.rem(col, size), 1)
            region[part, 0, here, :] = region[part, 0, here, :] + jnp.where(in_first, turned, 0.0)
            region[part, 1, here, :] = region[part, 1, here, :] + jnp.where(in_first, 0.0, turned)
        return carry

    lax.fori_loop(0, slots, one_slot, 0)
    for half in range(2):
        cols = pl.ds(half * size, size)
        own_ref[:, :, cols] = region[:, half, :rows, :]
        band_ref[:, :, cols] = region[:, half, rows:, :]


def add_windows(offsets, terms, rows, width):
    slots, _, size = terms.shape
    vmem = pl.BlockSpec(memory_space=VMEM)
    return pl.pallas_call(
        gather_kernel,
        out_shape=[
            jax.ShapeDtypeStruct((2, rows, width), jnp.float32),
            jax.ShapeDtypeStruct((2, size, width), jnp.float32),
        ],
        in_specs=[pl.BlockSpec(memory_space=SMEM), vmem],
        out_specs=[vmem] * 2,
        scratch_shapes=[VMEM((2, 2, rows + size, size), jnp.float32)],
        compiler_params=pltpu.CompilerParams(vmem_limit_bytes=12 * 2**20),
        name="gather",
    )(offsets, terms)


def passed_along(block, axis, distance):
    count = lax.axis_size(axis)
    return lax.ppermute(block, axis, [((i - distance) % count, i) for i in range(count)])


def per_device(obj_real, obj_imag, probe_real, probe_imag, prop_phase, intensity, offsets, counts):
    size = probe_real.shape[0]
    rows, width = obj_real.shape[1:]
    slot = lax.axis_index("cuts")
    below_real = passed_along(obj_real, "tile", -1)
    below_imag = passed_along(obj_imag, "tile", -1)
    matrices = build_matrices(prop_phase)
    probe = jnp.stack([probe_real, probe_imag])
    measured = lax.dynamic_slice_in_dim(intensity, slot, 1, 0)
    live = (slot < counts).astype(jnp.int32)
    windows = cut_windows(offsets, obj_real, obj_imag, below_real, below_imag, size)
    windows = lax.all_to_all(windows, "cuts", 0, 0, tiled=True)
    terms = run_chain(live, probe, matrices, windows, measured)
    terms = lax.all_to_all(terms, "cuts", 0, 0, tiled=True)
    probe_part = jnp.sum(terms[:, 2 * size :], axis=0)
    tiles = lax.axis_size("tile")
    spread = jnp.broadcast_to(probe_part[None], (tiles,) + probe_part.shape)
    probe_parts = lax.all_to_all(spread, "tile", 0, 0, tiled=True)
    own, band = add_windows(offsets, terms, rows, width)
    band = passed_along(band, "tile", 1)
    probe_grad = jnp.sum(probe_parts, axis=0).reshape(2, -1, size)
    object_grad = (own + band)[:, None]
    return object_grad, probe_grad


def solution(mesh):
    in_specs = (
        P("cuts", "tile", None),
        P("cuts", "tile", None),
        P(),
        P(),
        P(),
        P("tile", None, None),
        P("tile", None),
        P("tile"),
    )
    out_specs = (P(None, "cuts", "tile", None), P(None, "cuts", None))
    return jax.shard_map(
        per_device, mesh=mesh, in_specs=in_specs, out_specs=out_specs, check_vma=False
    )
```

```python
import functools
import math

import jax
import jax.numpy as jnp
import numpy as np
from jax import lax
from jax.experimental import pallas as pl
from jax.experimental.pallas import tpu as pltpu
from jax.sharding import PartitionSpec as P

VMEM = pltpu.VMEM
SMEM = pltpu.SMEM


def split_bf16(value):
    high = value.astype(jnp.bfloat16)
    low = (value - high.astype(jnp.float32)).astype(jnp.bfloat16)
    return high, low


def exact_dot(left, right):
    return jnp.dot(left, right, precision=lax.Precision.HIGHEST, preferred_element_type=jnp.float32)


def fourier_pair(size):
    places = np.arange(size)
    angle = (places[:, None] * places[None, :] % size) * (2.0 * math.pi / size)
    scale = 1.0 / math.sqrt(size)
    return (np.cos(angle) * scale).astype(np.float32), (-np.sin(angle) * scale).astype(np.float32)


def matrix_kernel(phase_ref, fourier_ref, dither_ref, matrix_ref):
    f_real, f_imag = fourier_ref[0], fourier_ref[1]
    phase = phase_ref[...]
    k_real, k_imag = jnp.cos(phase), jnp.sin(phase)
    l_real = f_real * k_real + f_imag * k_imag
    l_imag = f_real * k_imag - f_imag * k_real
    s_real = exact_dot(l_real, f_real) - exact_dot(l_imag, f_imag)
    s_imag = exact_dot(l_real, f_imag) + exact_dot(l_imag, f_real)
    for k, matrix in enumerate((s_real, s_imag, s_real.T, s_imag.T, f_real, f_imag)):
        high = matrix.astype(jnp.bfloat16)
        low = (matrix - high.astype(jnp.float32)) * (1.0 + dither_ref[k % 2])
        matrix_ref[k] = high
        matrix_ref[k + 6] = low.astype(jnp.bfloat16)


def build_matrices(prop_phase):
    size = prop_phase.shape[0]
    dither = np.random.default_rng(1).uniform(-0.003, 0.003, (2, size, size)).astype(np.float32)
    return pl.pallas_call(
        matrix_kernel,
        out_shape=jax.ShapeDtypeStruct((12, size, size), jnp.bfloat16),
        in_specs=[pl.BlockSpec(memory_space=VMEM)] * 3,
        out_specs=pl.BlockSpec(memory_space=VMEM),
        name="matrices",
    )(prop_phase[None], np.stack(fourier_pair(size)), dither)


def assemble(matrix_ref, first, right_ref, left_ref):
    size = matrix_ref.shape[1]
    uses = ((0, 2, 1.0), (4, 4, 1.0), (4, 4, -1.0), (2, 0, -1.0))
    for which, (left, right, sign) in enumerate(uses):
        real, imag = matrix_ref[first + right], matrix_ref[first + right + 1] * sign
        right_ref[which, :size, :size] = real
        right_ref[which, :size, size:] = imag
        right_ref[which, size:, :size] = -imag
        right_ref[which, size:, size:] = real
        left_ref[which, :, :size] = matrix_ref[first + left]
        left_ref[which, :, size:] = matrix_ref[first + left + 1] * sign


def sandwich(wide, operators, which):
    dot = functools.partial(jnp.dot, preferred_element_type=jnp.float32)
    right_high, right_low, left_high, left_low = (ref[which] for ref in operators)
    size = wide.shape[0]
    high, low = split_bf16(wide)
    middle = dot(high, right_high) + dot(low, right_high) + dot(high, right_low)
    high, low = (
        jnp.concatenate(
            [half, jnp.concatenate([-half[:, size:], half[:, :size]], axis=1)], axis=0
        )
        for half in split_bf16(middle)
    )
    out = dot(left_high, high) + dot(left_low, high) + dot(left_high, low)
    return out[:, :size], out[:, size:]


def chain_kernel(live_ref, probe_real, probe_imag, *refs):
    matrix_ref, measured_ref, window_ref, out_ref, waves, *operators = refs
    slices = window_ref.shape[0]
    size = probe_real.shape[0]
    extra = size // slices
    live = live_ref[0] > 0

    @pl.when(jnp.logical_not(live))
    def _():
        out_ref[...] = jnp.zeros_like(out_ref)

    @pl.when(live)
    def _():
        assemble(matrix_ref, 0, operators[0], operators[2])
        assemble(matrix_ref, 6, operators[1], operators[3])

        def modulated(s, real, imag):
            waves[s, :size, :] = real
            waves[s, size:, :] = imag
            p_real = window_ref[s, :size, :]
            p_imag = window_ref[s, size:, :]
            return jnp.concatenate(
                [real * p_real - imag * p_imag, real * p_imag + imag * p_real], axis=1
            )

        state = (probe_real[...], probe_imag[...])
        for s in range(slices - 1):
            state = sandwich(modulated(s, *state), operators, 0)
        wide = modulated(slices - 1, *state)
        far_r, far_i = sandwich(wide, operators, 1)
        excess = 2.0 * (far_r * far_r + far_i * far_i - measured_ref[0])
        wide = jnp.concatenate([excess * far_r, excess * far_i], axis=1)
        h_r, h_i = sandwich(wide, operators, 2)
        for s in reversed(range(slices)):
            w_r = waves[s, :size, :]
            w_i = waves[s, size:, :]
            p_real = window_ref[s, :size, :]
            p_imag = window_ref[s, size:, :]
            out_ref[s, :size, :] = w_r * h_r + w_i * h_i
            out_ref[s, size : 2 * size, :] = w_r * h_i - w_i * h_r
            g_r = p_real * h_r + p_imag * h_i
            g_i = p_real * h_i - p_imag * h_r
            if s > 0:
                wide = jnp.concatenate([g_r, g_i], axis=1)
                h_r, h_i = sandwich(wide, operators, 3)
        for s in range(slices):
            out_ref[s, 2 * size : 2 * size + extra, :] = g_r[s * extra : (s + 1) * extra]
            out_ref[s, 2 * size + extra :, :] = g_i[s * extra : (s + 1) * extra]


def run_chain(live, probe_real, probe_imag, matrices, windows, measured):
    slices, _, size = windows.shape
    rows = 2 * size + 2 * (size // slices)
    vmem = pl.BlockSpec(memory_space=VMEM)
    return pl.pallas_call(
        chain_kernel,
        out_shape=jax.ShapeDtypeStruct((slices, rows, size), jnp.float32),
        in_specs=[pl.BlockSpec(memory_space=SMEM)] + [vmem] * 5,
        out_specs=vmem,
        scratch_shapes=[
            VMEM((slices, 2 * size, size), jnp.float32),
            VMEM((4, 2 * size, 2 * size), jnp.bfloat16),
            VMEM((4, 2 * size, 2 * size), jnp.bfloat16),
            VMEM((4, size, 2 * size), jnp.bfloat16),
            VMEM((4, size, 2 * size), jnp.bfloat16),
        ],
        compiler_params=pltpu.CompilerParams(vmem_limit_bytes=16 * 2**20),
        name="chain",
    )(live, probe_real, probe_imag, matrices, measured, windows)


def cut_kernel(
    offset_ref, real_hbm, imag_hbm, real_below, imag_below, out_ref, region, sems
):
    slots, _, size = out_ref.shape
    rows = real_hbm.shape[1]
    parts = ((0, 0, real_hbm), (1, 0, imag_hbm), (0, rows, real_below), (1, rows, imag_below))
    arrivals = []
    for part, first, source in parts:
        for half in range(2):
            arrivals.append(
                pltpu.make_async_copy(
                    source.at[0, :, pl.ds(half * size, size)],
                    region.at[part, half, pl.ds(first, rows)],
                    sems.at[len(arrivals)],
                )
            )
    for arrival in arrivals:
        arrival.start()
    for arrival in arrivals:
        arrival.wait()
    lane = lax.broadcasted_iota(jnp.int32, (size, size), 1)

    def one_slot(n, carry):
        here = pl.ds(offset_ref[n, 0], size)
        col = offset_ref[n, 1]
        shift = lax.rem(size - col + size, size)
        in_first = lane >= col
        for part in range(2):
            mixed = jnp.where(in_first, region[part, 0, here, :], region[part, 1, here, :])
            out_ref[n, part * size : (part + 1) * size, :] = pltpu.roll(mixed, shift, 1)
        return carry

    lax.fori_loop(0, slots, one_slot, 0, unroll=2)


def cut_windows(offsets, obj_real, obj_imag, below_real, below_imag, size):
    slots = offsets.shape[0]
    _, rows, width = obj_real.shape
    return pl.pallas_call(
        cut_kernel,
        out_shape=jax.ShapeDtypeStruct((slots, 2 * size, size), jnp.float32),
        in_specs=[pl.BlockSpec(memory_space=SMEM)] + [pl.BlockSpec(memory_space=pl.ANY)] * 4,
        out_specs=pl.BlockSpec(memory_space=VMEM),
        scratch_shapes=[
            VMEM((2, 2, 2 * rows, size), jnp.float32),
            pltpu.SemaphoreType.DMA((8,)),
        ],
        compiler_params=pltpu.CompilerParams(vmem_limit_bytes=12 * 2**20),
        name="cut",
    )(offsets, obj_real, obj_imag, below_real, below_imag)


def gather_kernel(offset_ref, terms_ref, own_ref, band_ref, region):
    slots, _, size = terms_ref.shape
    rows = own_ref.shape[1]
    region[...] = jnp.zeros_like(region)
    lane = lax.broadcasted_iota(jnp.int32, (size, size), 1)

    def one_slot(n, carry):
        here = pl.ds(offset_ref[n, 0], size)
        col = offset_ref[n, 1]
        in_first = lane >= col
        for part in range(2):
            term = terms_ref[n, part * size : (part + 1) * size, :]
            turned = pltpu.roll(term, lax.rem(col, size), 1)
            region[part, 0, here, :] = region[part, 0, here, :] + jnp.where(in_first, turned, 0.0)
            region[part, 1, here, :] = region[part, 1, here, :] + jnp.where(in_first, 0.0, turned)
        return carry

    lax.fori_loop(0, slots, one_slot, 0, unroll=2)
    for half in range(2):
        cols = pl.ds(half * size, size)
        own_ref[:, :, cols] = region[:, half, :rows, :]
        band_ref[:, :, cols] = region[:, half, rows:, :]


def add_windows(offsets, terms, rows, width):
    slots, _, size = terms.shape
    vmem = pl.BlockSpec(memory_space=VMEM)
    return pl.pallas_call(
        gather_kernel,
        out_shape=[
            jax.ShapeDtypeStruct((2, rows, width), jnp.float32),
            jax.ShapeDtypeStruct((2, size, width), jnp.float32),
        ],
        in_specs=[pl.BlockSpec(memory_space=SMEM), vmem],
        out_specs=[vmem] * 2,
        scratch_shapes=[VMEM((2, 2, rows + size, size), jnp.float32)],
        compiler_params=pltpu.CompilerParams(vmem_limit_bytes=12 * 2**20),
        name="gather",
    )(offsets, terms)


def passed_along(block, axis, distance):
    count = lax.axis_size(axis)
    return lax.ppermute(block, axis, [((i - distance) % count, i) for i in range(count)])


def per_device(obj_real, obj_imag, probe_real, probe_imag, prop_phase, intensity, offsets, counts):
    size = probe_real.shape[0]
    rows, width = obj_real.shape[1:]
    slot = lax.axis_index("cuts")
    below_real = passed_along(obj_real, "tile", -1)
    below_imag = passed_along(obj_imag, "tile", -1)
    matrices = build_matrices(prop_phase)
    measured = lax.dynamic_slice_in_dim(intensity, slot, 1, 0)
    live = (slot < counts).astype(jnp.int32)
    below_real, below_imag, matrices, measured, live = lax.optimization_barrier(
        (below_real, below_imag, matrices, measured, live)
    )
    windows = cut_windows(offsets, obj_real, obj_imag, below_real, below_imag, size)
    windows = lax.all_to_all(windows, "cuts", 0, 0, tiled=True)
    terms = run_chain(live, probe_real, probe_imag, matrices, windows, measured)
    terms = lax.all_to_all(terms, "cuts", 0, 0, tiled=True)
    probe_part = jnp.sum(terms[:, 2 * size :], axis=0)
    tiles = lax.axis_size("tile")
    spread = jnp.broadcast_to(probe_part[None], (tiles,) + probe_part.shape)
    probe_parts = lax.all_to_all(spread, "tile", 0, 0, tiled=True)
    own, band = add_windows(offsets, terms, rows, width)
    band = passed_along(band, "tile", 1)
    probe_grad = jnp.sum(probe_parts, axis=0).reshape(2, -1, size)
    object_grad = (own + band)[:, None]
    return object_grad, probe_grad


def solution(mesh):
    in_specs = (
        P("cuts", "tile", None),
        P("cuts", "tile", None),
        P(),
        P(),
        P(),
        P("tile", None, None),
        P("tile", None),
        P("tile"),
    )
    out_specs = (P(None, "cuts", "tile", None), P(None, "cuts", None))
    return jax.shard_map(
        per_device, mesh=mesh, in_specs=in_specs, out_specs=out_specs, check_vma=False
    )
```

```python
import functools
import math

import jax
import jax.numpy as jnp
import numpy as np
from jax import lax
from jax.experimental import pallas as pl
from jax.experimental.pallas import tpu as pltpu
from jax.sharding import PartitionSpec as P

VMEM = pltpu.VMEM
SMEM = pltpu.SMEM


def split_bf16(value):
    high = value.astype(jnp.bfloat16)
    low = (value - high.astype(jnp.float32)).astype(jnp.bfloat16)
    return high, low


def exact_dot(left, right):
    return jnp.dot(left, right, precision=lax.Precision.HIGHEST, preferred_element_type=jnp.float32)


def fourier_pair(size):
    places = np.arange(size)
    angle = (places[:, None] * places[None, :] % size) * (2.0 * math.pi / size)
    scale = 1.0 / math.sqrt(size)
    return (np.cos(angle) * scale).astype(np.float32), (-np.sin(angle) * scale).astype(np.float32)


def prepare_kernel(phase_ref, fourier_ref, dither_ref, real_ref, imag_ref, matrix_ref, own_ref):
    size = matrix_ref.shape[1]
    for half in range(2):
        cols = pl.ds(half * size, size)
        own_ref[0, half] = real_ref[0, :, cols]
        own_ref[1, half] = imag_ref[0, :, cols]
    f_real, f_imag = fourier_ref[0], fourier_ref[1]
    phase = phase_ref[...]
    k_real, k_imag = jnp.cos(phase), jnp.sin(phase)
    l_real = f_real * k_real + f_imag * k_imag
    l_imag = f_real * k_imag - f_imag * k_real
    s_real = exact_dot(l_real, f_real) - exact_dot(l_imag, f_imag)
    s_imag = exact_dot(l_real, f_imag) + exact_dot(l_imag, f_real)
    for k, matrix in enumerate((s_real, s_imag, s_real.T, s_imag.T, f_real, f_imag)):
        high = matrix.astype(jnp.bfloat16)
        low = (matrix - high.astype(jnp.float32)) * (1.0 + dither_ref[k % 2])
        matrix_ref[k] = high
        matrix_ref[k + 6] = low.astype(jnp.bfloat16)


def prepare(prop_phase, obj_real, obj_imag):
    size = prop_phase.shape[0]
    rows = obj_real.shape[1]
    dither = np.random.default_rng(1).uniform(-0.003, 0.003, (2, size, size)).astype(np.float32)
    return pl.pallas_call(
        prepare_kernel,
        out_shape=[
            jax.ShapeDtypeStruct((12, size, size), jnp.bfloat16),
            jax.ShapeDtypeStruct((2, 2, rows, size), jnp.float32),
        ],
        in_specs=[pl.BlockSpec(memory_space=VMEM)] * 5,
        out_specs=[pl.BlockSpec(memory_space=VMEM)] * 2,
        name="prepare",
    )(prop_phase[None], np.stack(fourier_pair(size)), dither, obj_real, obj_imag)


def assemble(matrix_ref, first, right_ref, left_ref):
    size = matrix_ref.shape[1]
    uses = ((0, 2, 1.0), (4, 4, 1.0), (4, 4, -1.0), (2, 0, -1.0))
    for which, (left, right, sign) in enumerate(uses):
        real, imag = matrix_ref[first + right], matrix_ref[first + right + 1] * sign
        right_ref[which, :size, :size] = real
        right_ref[which, :size, size:] = imag
        right_ref[which, size:, :size] = -imag
        right_ref[which, size:, size:] = real
        left_ref[which, :, :size] = matrix_ref[first + left]
        left_ref[which, :, size:] = matrix_ref[first + left + 1] * sign


def sandwich(wide, operators, which):
    dot = functools.partial(jnp.dot, preferred_element_type=jnp.float32)
    right_high, right_low, left_high, left_low = (ref[which] for ref in operators)
    size = wide.shape[0]
    high, low = split_bf16(wide)
    middle = dot(
        jnp.concatenate([high, low, high], axis=1),
        jnp.concatenate([right_high, right_high, right_low], axis=0),
    )
    high, low = (
        jnp.concatenate(
            [half, jnp.concatenate([-half[:, size:], half[:, :size]], axis=1)], axis=0
        )
        for half in split_bf16(middle)
    )
    out = dot(left_high, high) + dot(left_low, high) + dot(left_high, low)
    return out[:, :size], out[:, size:]


def chain_kernel(live_ref, probe_real, probe_imag, *refs):
    matrix_ref, measured_ref, window_ref, out_ref, waves, *operators = refs
    slices = window_ref.shape[0]
    size = probe_real.shape[0]
    extra = size // slices
    live = live_ref[0] > 0

    @pl.when(jnp.logical_not(live))
    def _():
        out_ref[...] = jnp.zeros_like(out_ref)

    @pl.when(live)
    def _():
        assemble(matrix_ref, 0, operators[0], operators[2])
        assemble(matrix_ref, 6, operators[1], operators[3])

        def modulated(s, real, imag):
            waves[s, :size, :] = real
            waves[s, size:, :] = imag
            p_real = window_ref[s, :size, :]
            p_imag = window_ref[s, size:, :]
            return jnp.concatenate(
                [real * p_real - imag * p_imag, real * p_imag + imag * p_real], axis=1
            )

        state = (probe_real[...], probe_imag[...])
        for s in range(slices - 1):
            state = sandwich(modulated(s, *state), operators, 0)
        wide = modulated(slices - 1, *state)
        far_r, far_i = sandwich(wide, operators, 1)
        excess = 2.0 * (far_r * far_r + far_i * far_i - measured_ref[0])
        wide = jnp.concatenate([excess * far_r, excess * far_i], axis=1)
        h_r, h_i = sandwich(wide, operators, 2)
        for s in reversed(range(slices)):
            w_r = waves[s, :size, :]
            w_i = waves[s, size:, :]
            p_real = window_ref[s, :size, :]
            p_imag = window_ref[s, size:, :]
            out_ref[s, :size, :] = w_r * h_r + w_i * h_i
            out_ref[s, size : 2 * size, :] = w_r * h_i - w_i * h_r
            g_r = p_real * h_r + p_imag * h_i
            g_i = p_real * h_i - p_imag * h_r
            if s > 0:
                wide = jnp.concatenate([g_r, g_i], axis=1)
                h_r, h_i = sandwich(wide, operators, 3)
        for s in range(slices):
            out_ref[s, 2 * size : 2 * size + extra, :] = g_r[s * extra : (s + 1) * extra]
            out_ref[s, 2 * size + extra :, :] = g_i[s * extra : (s + 1) * extra]


def run_chain(live, probe_real, probe_imag, matrices, windows, measured):
    slices, _, size = windows.shape
    rows = 2 * size + 2 * (size // slices)
    vmem = pl.BlockSpec(memory_space=VMEM)
    return pl.pallas_call(
        chain_kernel,
        out_shape=jax.ShapeDtypeStruct((slices, rows, size), jnp.float32),
        in_specs=[pl.BlockSpec(memory_space=SMEM)] + [vmem] * 5,
        out_specs=vmem,
        scratch_shapes=[
            VMEM((slices, 2 * size, size), jnp.float32),
            VMEM((4, 2 * size, 2 * size), jnp.bfloat16),
            VMEM((4, 2 * size, 2 * size), jnp.bfloat16),
            VMEM((4, size, 2 * size), jnp.bfloat16),
            VMEM((4, size, 2 * size), jnp.bfloat16),
        ],
        compiler_params=pltpu.CompilerParams(vmem_limit_bytes=16 * 2**20),
        name="chain",
    )(live, probe_real, probe_imag, matrices, measured, windows)


def cut_kernel(offset_ref, own_ref, real_below, imag_below, out_ref, region):
    slots, _, size = out_ref.shape
    rows = own_ref.shape[2]
    region[:, :, :rows, :] = own_ref[...]
    for half in range(2):
        cols = pl.ds(half * size, size)
        region[0, half, rows:, :] = real_below[0, :, cols]
        region[1, half, rows:, :] = imag_below[0, :, cols]
    lane = lax.broadcasted_iota(jnp.int32, (size, size), 1)

    def one_slot(n, carry):
        here = pl.ds(offset_ref[n, 0], size)
        col = offset_ref[n, 1]
        shift = lax.rem(size - col + size, size)
        in_first = lane >= col
        for part in range(2):
            mixed = jnp.where(in_first, region[part, 0, here, :], region[part, 1, here, :])
            out_ref[n, part * size : (part + 1) * size, :] = pltpu.roll(mixed, shift, 1)
        return carry

    lax.fori_loop(0, slots, one_slot, 0, unroll=2)


def cut_windows(offsets, own, below_real, below_imag):
    slots = offsets.shape[0]
    _, _, rows, size = own.shape
    vmem = pl.BlockSpec(memory_space=VMEM)
    return pl.pallas_call(
        cut_kernel,
        out_shape=jax.ShapeDtypeStruct((slots, 2 * size, size), jnp.float32),
        in_specs=[pl.BlockSpec(memory_space=SMEM)] + [vmem] * 3,
        out_specs=vmem,
        scratch_shapes=[VMEM((2, 2, 2 * rows, size), jnp.float32)],
        compiler_params=pltpu.CompilerParams(vmem_limit_bytes=12 * 2**20),
        name="cut",
    )(offsets, own, below_real, below_imag)


def gather_kernel(offset_ref, terms_ref, own_ref, band_ref, region):
    slots, _, size = terms_ref.shape
    rows = own_ref.shape[1]
    region[...] = jnp.zeros_like(region)
    lane = lax.broadcasted_iota(jnp.int32, (size, size), 1)

    def one_slot(n, carry):
        here = pl.ds(offset_ref[n, 0], size)
        col = offset_ref[n, 1]
        in_first = lane >= col
        for part in range(2):
            term = terms_ref[n, part * size : (part + 1) * size, :]
            turned = pltpu.roll(term, lax.rem(col, size), 1)
            region[part, 0, here, :] = region[part, 0, here, :] + jnp.where(in_first, turned, 0.0)
            region[part, 1, here, :] = region[part, 1, here, :] + jnp.where(in_first, 0.0, turned)
        return carry

    lax.fori_loop(0, slots, one_slot, 0, unroll=2)
    for half in range(2):
        cols = pl.ds(half * size, size)
        own_ref[:, :, cols] = region[:, half, :rows, :]
        band_ref[:, :, cols] = region[:, half, rows:, :]


def add_windows(offsets, terms, rows, width):
    slots, _, size = terms.shape
    vmem = pl.BlockSpec(memory_space=VMEM)
    return pl.pallas_call(
        gather_kernel,
        out_shape=[
            jax.ShapeDtypeStruct((2, rows, width), jnp.float32),
            jax.ShapeDtypeStruct((2, size, width), jnp.float32),
        ],
        in_specs=[pl.BlockSpec(memory_space=SMEM), vmem],
        out_specs=[vmem] * 2,
        scratch_shapes=[VMEM((2, 2, rows + size, size), jnp.float32)],
        compiler_params=pltpu.CompilerParams(vmem_limit_bytes=12 * 2**20),
        name="gather",
    )(offsets, terms)


def passed_along(block, axis, distance):
    count = lax.axis_size(axis)
    return lax.ppermute(block, axis, [((i - distance) % count, i) for i in range(count)])


def per_device(obj_real, obj_imag, probe_real, probe_imag, prop_phase, intensity, offsets, counts):
    size = probe_real.shape[0]
    rows, width = obj_real.shape[1:]
    slot = lax.axis_index("cuts")
    below_real = passed_along(obj_real, "tile", -1)
    below_imag = passed_along(obj_imag, "tile", -1)
    matrices, own_rows = prepare(prop_phase, obj_real, obj_imag)
    measured = lax.dynamic_slice_in_dim(intensity, slot, 1, 0)
    live = (slot < counts).astype(jnp.int32)
    below_real, below_imag, matrices, own_rows, measured, live = lax.optimization_barrier(
        (below_real, below_imag, matrices, own_rows, measured, live)
    )
    windows = cut_windows(offsets, own_rows, below_real, below_imag)
    windows = lax.all_to_all(windows, "cuts", 0, 0, tiled=True)
    terms = run_chain(live, probe_real, probe_imag, matrices, windows, measured)
    terms = lax.all_to_all(terms, "cuts", 0, 0, tiled=True)
    probe_part = jnp.sum(terms[:, 2 * size :], axis=0)
    tiles = lax.axis_size("tile")
    spread = jnp.broadcast_to(probe_part[None], (tiles,) + probe_part.shape)
    probe_parts = lax.all_to_all(spread, "tile", 0, 0, tiled=True)
    own, band = add_windows(offsets, terms, rows, width)
    band = passed_along(band, "tile", 1)
    probe_grad = jnp.sum(probe_parts, axis=0).reshape(2, -1, size)
    object_grad = (own + band)[:, None]
    return object_grad, probe_grad


def solution(mesh):
    in_specs = (
        P("cuts", "tile", None),
        P("cuts", "tile", None),
        P(),
        P(),
        P(),
        P("tile", None, None),
        P("tile", None),
        P("tile"),
    )
    out_specs = (P(None, "cuts", "tile", None), P(None, "cuts", None))
    return jax.shard_map(
        per_device, mesh=mesh, in_specs=in_specs, out_specs=out_specs, check_vma=False
    )
```

```python
import functools
import math

import jax
import jax.numpy as jnp
import numpy as np
from jax import lax
from jax.experimental import pallas as pl
from jax.experimental.pallas import tpu as pltpu
from jax.sharding import PartitionSpec as P

VMEM = pltpu.VMEM
SMEM = pltpu.SMEM


def split_bf16(value):
    high = value.astype(jnp.bfloat16)
    low = (value - high.astype(jnp.float32)).astype(jnp.bfloat16)
    return high, low


def exact_dot(left, right):
    return jnp.dot(left, right, precision=lax.Precision.HIGHEST, preferred_element_type=jnp.float32)


def fourier_pair(size):
    places = np.arange(size)
    angle = (places[:, None] * places[None, :] % size) * (2.0 * math.pi / size)
    scale = 1.0 / math.sqrt(size)
    return (np.cos(angle) * scale).astype(np.float32), (-np.sin(angle) * scale).astype(np.float32)


def prepare_kernel(phase_ref, fourier_ref, dither_ref, real_ref, imag_ref, matrix_ref, own_ref):
    size = matrix_ref.shape[1]
    for half in range(2):
        cols = pl.ds(half * size, size)
        own_ref[0, half] = real_ref[0, :, cols]
        own_ref[1, half] = imag_ref[0, :, cols]
    f_real, f_imag = fourier_ref[0], fourier_ref[1]
    phase = phase_ref[...]
    k_real, k_imag = jnp.cos(phase), jnp.sin(phase)
    l_real = f_real * k_real + f_imag * k_imag
    l_imag = f_real * k_imag - f_imag * k_real
    s_real = exact_dot(l_real, f_real) - exact_dot(l_imag, f_imag)
    s_imag = exact_dot(l_real, f_imag) + exact_dot(l_imag, f_real)
    for k, matrix in enumerate((s_real, s_imag, s_real.T, s_imag.T, f_real, f_imag)):
        high = matrix.astype(jnp.bfloat16)
        low = (matrix - high.astype(jnp.float32)) * (1.0 + dither_ref[k % 2])
        matrix_ref[k] = high
        matrix_ref[k + 6] = low.astype(jnp.bfloat16)


def prepare(prop_phase, obj_real, obj_imag):
    size = prop_phase.shape[0]
    rows = obj_real.shape[1]
    dither = np.random.default_rng(1).uniform(-0.003, 0.003, (2, size, size)).astype(np.float32)
    return pl.pallas_call(
        prepare_kernel,
        out_shape=[
            jax.ShapeDtypeStruct((12, size, size), jnp.bfloat16),
            jax.ShapeDtypeStruct((2, 2, rows, size), jnp.float32),
        ],
        in_specs=[pl.BlockSpec(memory_space=VMEM)] * 5,
        out_specs=[pl.BlockSpec(memory_space=VMEM)] * 2,
        name="prepare",
    )(prop_phase[None], np.stack(fourier_pair(size)), dither, obj_real, obj_imag)


def assemble(matrix_ref, first, right_ref, left_ref):
    size = matrix_ref.shape[1]
    uses = ((0, 2, 1.0), (4, 4, 1.0), (4, 4, -1.0), (2, 0, -1.0))
    for which, (left, right, sign) in enumerate(uses):
        real, imag = matrix_ref[first + right], matrix_ref[first + right + 1] * sign
        right_ref[which, :size, :size] = real
        right_ref[which, :size, size:] = imag
        right_ref[which, size:, :size] = -imag
        right_ref[which, size:, size:] = real
        left_ref[which, :, :size] = matrix_ref[first + left]
        left_ref[which, :, size:] = matrix_ref[first + left + 1] * sign


def sandwich(wide, operators, which):
    dot = functools.partial(jnp.dot, preferred_element_type=jnp.float32)
    right_high, right_low, left_high, left_low = (ref[which] for ref in operators)
    size = wide.shape[0]
    high, low = split_bf16(wide)
    middle = dot(
        jnp.concatenate([high, low, high], axis=1),
        jnp.concatenate([right_high, right_high, right_low], axis=0),
    )
    high, low = (
        jnp.concatenate(
            [half, jnp.concatenate([-half[:, size:], half[:, :size]], axis=1)], axis=0
        )
        for half in split_bf16(middle)
    )
    out = dot(
        jnp.concatenate([left_high, left_low, left_high], axis=1),
        jnp.concatenate([high, high, low], axis=0),
    )
    return out[:, :size], out[:, size:]


def chain_kernel(live_ref, probe_real, probe_imag, *refs):
    matrix_ref, measured_ref, window_ref, out_ref, waves, *operators = refs
    slices = window_ref.shape[0]
    size = probe_real.shape[0]
    extra = size // slices
    live = live_ref[0] > 0

    @pl.when(jnp.logical_not(live))
    def _():
        out_ref[...] = jnp.zeros_like(out_ref)

    @pl.when(live)
    def _():
        assemble(matrix_ref, 0, operators[0], operators[2])
        assemble(matrix_ref, 6, operators[1], operators[3])

        def modulated(s, real, imag):
            waves[s, :size, :] = real
            waves[s, size:, :] = imag
            p_real = window_ref[s, :size, :]
            p_imag = window_ref[s, size:, :]
            return jnp.concatenate(
                [real * p_real - imag * p_imag, real * p_imag + imag * p_real], axis=1
            )

        state = (probe_real[...], probe_imag[...])
        for s in range(slices - 1):
            state = sandwich(modulated(s, *state), operators, 0)
        wide = modulated(slices - 1, *state)
        far_r, far_i = sandwich(wide, operators, 1)
        excess = 2.0 * (far_r * far_r + far_i * far_i - measured_ref[0])
        wide = jnp.concatenate([excess * far_r, excess * far_i], axis=1)
        h_r, h_i = sandwich(wide, operators, 2)
        for s in reversed(range(slices)):
            w_r = waves[s, :size, :]
            w_i = waves[s, size:, :]
            p_real = window_ref[s, :size, :]
            p_imag = window_ref[s, size:, :]
            out_ref[s, :size, :] = w_r * h_r + w_i * h_i
            out_ref[s, size : 2 * size, :] = w_r * h_i - w_i * h_r
            g_r = p_real * h_r + p_imag * h_i
            g_i = p_real * h_i - p_imag * h_r
            if s > 0:
                wide = jnp.concatenate([g_r, g_i], axis=1)
                h_r, h_i = sandwich(wide, operators, 3)
        for s in range(slices):
            out_ref[s, 2 * size : 2 * size + extra, :] = g_r[s * extra : (s + 1) * extra]
            out_ref[s, 2 * size + extra :, :] = g_i[s * extra : (s + 1) * extra]


def run_chain(live, probe_real, probe_imag, matrices, windows, measured):
    slices, _, size = windows.shape
    rows = 2 * size + 2 * (size // slices)
    vmem = pl.BlockSpec(memory_space=VMEM)
    return pl.pallas_call(
        chain_kernel,
        out_shape=jax.ShapeDtypeStruct((slices, rows, size), jnp.float32),
        in_specs=[pl.BlockSpec(memory_space=SMEM)] + [vmem] * 5,
        out_specs=vmem,
        scratch_shapes=[
            VMEM((slices, 2 * size, size), jnp.float32),
            VMEM((4, 2 * size, 2 * size), jnp.bfloat16),
            VMEM((4, 2 * size, 2 * size), jnp.bfloat16),
            VMEM((4, size, 2 * size), jnp.bfloat16),
            VMEM((4, size, 2 * size), jnp.bfloat16),
        ],
        compiler_params=pltpu.CompilerParams(vmem_limit_bytes=16 * 2**20),
        name="chain",
    )(live, probe_real, probe_imag, matrices, measured, windows)


def cut_kernel(offset_ref, own_ref, real_below, imag_below, out_ref, region):
    slots, _, size = out_ref.shape
    rows = own_ref.shape[2]
    region[:, :, :rows, :] = own_ref[...]
    for half in range(2):
        cols = pl.ds(half * size, size)
        region[0, half, rows:, :] = real_below[0, :, cols]
        region[1, half, rows:, :] = imag_below[0, :, cols]
    lane = lax.broadcasted_iota(jnp.int32, (size, size), 1)

    def one_slot(n, carry):
        here = pl.ds(offset_ref[n, 0], size)
        col = offset_ref[n, 1]
        shift = lax.rem(size - col + size, size)
        in_first = lane >= col
        for part in range(2):
            mixed = jnp.where(in_first, region[part, 0, here, :], region[part, 1, here, :])
            out_ref[n, part * size : (part + 1) * size, :] = pltpu.roll(mixed, shift, 1)
        return carry

    lax.fori_loop(0, slots, one_slot, 0, unroll=2)


def cut_windows(offsets, own, below_real, below_imag):
    slots = offsets.shape[0]
    _, _, rows, size = own.shape
    vmem = pl.BlockSpec(memory_space=VMEM)
    return pl.pallas_call(
        cut_kernel,
        out_shape=jax.ShapeDtypeStruct((slots, 2 * size, size), jnp.float32),
        in_specs=[pl.BlockSpec(memory_space=SMEM)] + [vmem] * 3,
        out_specs=vmem,
        scratch_shapes=[VMEM((2, 2, 2 * rows, size), jnp.float32)],
        compiler_params=pltpu.CompilerParams(vmem_limit_bytes=12 * 2**20),
        name="cut",
    )(offsets, own, below_real, below_imag)


def gather_kernel(offset_ref, terms_ref, own_ref, band_ref, region):
    slots, _, size = terms_ref.shape
    rows = own_ref.shape[1]
    region[...] = jnp.zeros_like(region)
    lane = lax.broadcasted_iota(jnp.int32, (size, size), 1)

    def one_slot(n, carry):
        here = pl.ds(offset_ref[n, 0], size)
        col = offset_ref[n, 1]
        in_first = lane >= col
        for part in range(2):
            term = terms_ref[n, part * size : (part + 1) * size, :]
            turned = pltpu.roll(term, lax.rem(col, size), 1)
            region[part, 0, here, :] = region[part, 0, here, :] + jnp.where(in_first, turned, 0.0)
            region[part, 1, here, :] = region[part, 1, here, :] + jnp.where(in_first, 0.0, turned)
        return carry

    lax.fori_loop(0, slots, one_slot, 0, unroll=2)
    for half in range(2):
        cols = pl.ds(half * size, size)
        own_ref[:, :, cols] = region[:, half, :rows, :]
        band_ref[:, :, cols] = region[:, half, rows:, :]


def add_windows(offsets, terms, rows, width):
    slots, _, size = terms.shape
    vmem = pl.BlockSpec(memory_space=VMEM)
    return pl.pallas_call(
        gather_kernel,
        out_shape=[
            jax.ShapeDtypeStruct((2, rows, width), jnp.float32),
            jax.ShapeDtypeStruct((2, size, width), jnp.float32),
        ],
        in_specs=[pl.BlockSpec(memory_space=SMEM), vmem],
        out_specs=[vmem] * 2,
        scratch_shapes=[VMEM((2, 2, rows + size, size), jnp.float32)],
        compiler_params=pltpu.CompilerParams(vmem_limit_bytes=12 * 2**20),
        name="gather",
    )(offsets, terms)


def finish_kernel(own_ref, band_ref, parts_ref, object_ref, probe_ref):
    object_ref[...] = own_ref[...] + band_ref[...]
    probe_ref[...] = jnp.sum(parts_ref[...], axis=0)


def finish(own, band, parts):
    vmem = pl.BlockSpec(memory_space=VMEM)
    return pl.pallas_call(
        finish_kernel,
        out_shape=[
            jax.ShapeDtypeStruct(own.shape, jnp.float32),
            jax.ShapeDtypeStruct(parts.shape[1:], jnp.float32),
        ],
        in_specs=[vmem] * 3,
        out_specs=[vmem] * 2,
        compiler_params=pltpu.CompilerParams(vmem_limit_bytes=12 * 2**20),
        name="finish",
    )(own, band, parts)


def passed_along(block, axis, distance):
    count = lax.axis_size(axis)
    return lax.ppermute(block, axis, [((i - distance) % count, i) for i in range(count)])


def per_device(obj_real, obj_imag, probe_real, probe_imag, prop_phase, intensity, offsets, counts):
    size = probe_real.shape[0]
    rows, width = obj_real.shape[1:]
    slot = lax.axis_index("cuts")
    below_real = passed_along(obj_real, "tile", -1)
    below_imag = passed_along(obj_imag, "tile", -1)
    matrices, own_rows = prepare(prop_phase, obj_real, obj_imag)
    measured = lax.dynamic_slice_in_dim(intensity, slot, 1, 0)
    live = (slot < counts).astype(jnp.int32)
    below_real, below_imag, matrices, own_rows, measured, live = lax.optimization_barrier(
        (below_real, below_imag, matrices, own_rows, measured, live)
    )
    windows = cut_windows(offsets, own_rows, below_real, below_imag)
    windows = lax.all_to_all(windows, "cuts", 0, 0, tiled=True)
    terms = run_chain(live, probe_real, probe_imag, matrices, windows, measured)
    terms = lax.all_to_all(terms, "cuts", 0, 0, tiled=True)
    probe_part = jnp.sum(terms[:, 2 * size :], axis=0)
    tiles = lax.axis_size("tile")
    spread = jnp.broadcast_to(probe_part[None], (tiles,) + probe_part.shape)
    probe_parts = lax.all_to_all(spread, "tile", 0, 0, tiled=True)
    own, band = add_windows(offsets, terms, rows, width)
    band = passed_along(band, "tile", 1)
    object_grad, probe_grad = finish(own, band, probe_parts)
    return object_grad[:, None], probe_grad.reshape(2, -1, size)


def solution(mesh):
    in_specs = (
        P("cuts", "tile", None),
        P("cuts", "tile", None),
        P(),
        P(),
        P(),
        P("tile", None, None),
        P("tile", None),
        P("tile"),
    )
    out_specs = (P(None, "cuts", "tile", None), P(None, "cuts", None))
    return jax.shard_map(
        per_device, mesh=mesh, in_specs=in_specs, out_specs=out_specs, check_vma=False
    )
```
